1024 devices in a mesh: island: 4 (over x_hi, core), fsdp: 16 (over z), tensor: 16 (over x_lo, y).
Axes of the slice: x: 4 (x_hi: 2, x_lo: 2; x = x_hi * 2 + x_lo), y: 8, z: 16, core: 2. Of those that a mesh axis runs over, the one named last changes fastest.
Arguments:
- tokens: bfloat16 [16384, 4608], P(('island', 'fsdp')), may hold values from -6 to 6
- cotangent: bfloat16 [16384, 4608], P(('island', 'fsdp')), may hold values from -0.19921875 to 0.19921875
- gate_tiles: bfloat16 [64, 16, 128, 128], P('fsdp', 'tensor'), may hold values from -0.25 to 0.25
- up_tiles: bfloat16 [64, 16, 128, 128], P('fsdp', 'tensor'), may hold values from -0.25 to 0.25
- gate_where: int32 [64, 16], P('fsdp', 'tensor'), may hold values from 0 to 647, as said below
- up_where: int32 [64, 16], P('fsdp', 'tensor'), may hold values from 0 to 647, as said below
- down_where: int32 [64, 16], P(None, 'tensor'), may hold values from 0 to 647, as said below
- down_global: float32 [64, 16, 128, 128], P('fsdp', 'tensor'), may hold values from -6 to 6
- down_moment: float32 [64, 16, 128, 128], P('fsdp', 'tensor'), may hold values from -3 to 3
Outputs:
- new_global: float32 [64, 16, 128, 128], P('fsdp', 'tensor')
- new_moment: float32 [64, 16, 128, 128], P('fsdp', 'tensor')
The draws below stay inside these ranges and needn't reach their ends.
Inputs may be any that keep to these rules, and one draw needn't show every extreme that they name: In each column t, the 64 entries of gate_where are distinct cells r * 18 + c of the 36 x 18 tile grid of shard t (r a block of the model width, c a block of the shard's hidden units). In each column t, the 64 entries of up_where are distinct cells r * 18 + c of the 36 x 18 tile grid of shard t. In each column t, the 64 entries of down_where are distinct cells a * 36 + b, a a block of shard t's hidden units (18 of them) and b a block of the model width.
All inputs are finite; a program needn't handle non-finite values.
Results may differ from the reference program's by a relative error of at most 0.00057.
Values may be sent and summed in bfloat16 or wider, within the bound.
No kernel may reach another device: no remote copies, remote signals or barrier semaphores. Data moves between devices by JAX's collectives and lax.ppermute only.
A program may use at most 128 MiB of HBM per device.

```python
import jax
import jax.numpy as jnp
from jax import lax

D = 4608
TILE = 128
DROWS = 36
FCOLS = 18
SHARDS = 16
KEPT = 64
ISLANDS = 4
ITOK = 4096
TOKENS = 16384


def pick_cells(key, cells):
    keys = jax.random.split(key, SHARDS + 3)

    def one_column(column_key):
        return jax.random.permutation(column_key, cells)[:KEPT]
    chosen = jax.vmap(one_column)(keys[:SHARDS])
    inner = 1 + jax.random.permutation(keys[SHARDS], cells - 2)[:KEPT - 2]
    ends = jnp.array([0, cells - 1], dtype=jnp.int32)
    special = jax.random.permutation(keys[SHARDS + 1], jnp.concatenate([ends, inner.astype(jnp.int32)]))
    column_at = jax.random.randint(keys[SHARDS + 2], (), 0, SHARDS)
    is_special = (jnp.arange(SHARDS, dtype=jnp.int32) == column_at)[:, None]
    chosen = jnp.where(is_special, special[None, :], chosen.astype(jnp.int32))
    return jnp.transpose(chosen).astype(jnp.int32)


def draw_gate_where(key, part):
    key = jax.random.fold_in(key, 11)
    return pick_cells(key, DROWS * FCOLS)


def draw_up_where(key, part):
    key = jax.random.fold_in(key, 12)
    return pick_cells(key, DROWS * FCOLS)


def draw_down_where(key, part):
    key = jax.random.fold_in(key, 13)
    return pick_cells(key, DROWS * FCOLS)


def levels(own_key, shape, cuts, low, top_value):
    def one(dim, shards_of):
        heights = jax.random.uniform(jax.random.fold_in(jax.random.fold_in(own_key, 6), dim), (shards_of,), jnp.float32, low / len(cuts), top_value / len(cuts))
        return jnp.repeat(jnp.exp(heights), shape[dim] // shards_of).reshape((-1,) + (1,) * (len(shape) - dim - 1))

    gain = one(*cuts[0])
    for cut in cuts[1:]:
        gain = gain * one(*cut)
    return gain


def noise(rng, dims, spread, bound, shards=(), held_as=jnp.bfloat16):
    values = spread * jax.random.normal(rng, dims, jnp.float32)
    if shards:
        values = values * levels(rng, dims, shards, -0.22, 0.18)
    return jnp.clip(values, -bound, bound).astype(held_as)


def setup_inputs(seed: int = 0) -> dict:
    streams_of = jax.random.split(jax.random.key(seed), 10)
    tokens = noise(streams_of[0], (TOKENS, D), 1.0, 6.0, ((0, 64),))
    cotangent = noise(streams_of[1], (TOKENS, D), 0.03125, 0.19921875, ((0, 64),))
    gate_tiles = noise(streams_of[2], (KEPT, SHARDS, TILE, TILE), (TILE * KEPT // FCOLS) ** -0.5, 0.25, ((0, 16), (1, 16)))
    up_tiles = noise(streams_of[3], (KEPT, SHARDS, TILE, TILE), (TILE * KEPT // FCOLS) ** -0.5, 0.25, ((0, 16), (1, 16)))
    gate_where = draw_gate_where(jax.random.fold_in(streams_of[9], 71), 0)
    up_where = draw_up_where(jax.random.fold_in(streams_of[9], 71), 0)
    down_where = draw_down_where(jax.random.fold_in(streams_of[9], 71), 0)
    down_global = noise(streams_of[7], (KEPT, SHARDS, TILE, TILE), 1.0, 6.0, ((0, 16), (1, 16)), jnp.float32)
    down_moment = noise(streams_of[8], (KEPT, SHARDS, TILE, TILE), 0.5, 3.0, ((0, 16), (1, 16)), jnp.float32)
    return {"tokens": tokens, "cotangent": cotangent, "gate_tiles": gate_tiles, "up_tiles": up_tiles, "gate_where": gate_where, "up_where": up_where, "down_where": down_where, "down_global": down_global, "down_moment": down_moment}


inner_rate = 0.5
decay_rate = 0.1
outer_rate = 0.7
momentum_rate = 0.9


def tile_project(tok_blocks, tiles, where, col_blocks):
    row_ids = where // col_blocks
    col_ids = where % col_blocks
    picked = jnp.take(tok_blocks, row_ids, axis=1).astype(jnp.float32)
    partial_value = jnp.einsum('tkr,krc->tkc', picked, tiles.astype(jnp.float32))
    onehot = (col_ids[:, None] == jnp.arange(col_blocks, dtype=jnp.int32)[None, :]).astype(jnp.float32)
    return jnp.einsum('tkc,kj->tjc', partial_value, onehot, precision=lax.Precision.HIGHEST)


def reference(tokens, cotangent, gate_tiles, up_tiles, gate_where, up_where, down_where, down_global, down_moment):
    tok_blocks = tokens.reshape(ISLANDS, ITOK, DROWS, TILE)
    cot_blocks = cotangent.reshape(ISLANDS, ITOK, DROWS, TILE)

    def one_shard(inputs):
        gate_part, up_part, gate_at, up_at, down_at, master, moment = inputs
        island_total = jnp.zeros((KEPT, TILE, TILE), jnp.float32)
        for island in range(ISLANDS):
            gate_sum = tile_project(tok_blocks[island], gate_part, gate_at, FCOLS)
            up_sum = tile_project(tok_blocks[island], up_part, up_at, FCOLS)
            hidden = (jax.nn.silu(gate_sum) * up_sum).astype(jnp.bfloat16)
            hidden_pick = jnp.take(hidden, down_at // DROWS, axis=1).astype(jnp.float32)
            cot_pick = jnp.take(cot_blocks[island], down_at % DROWS, axis=1).astype(jnp.float32)
            grad_tiles = jnp.einsum('tka,tkb->kab', hidden_pick, cot_pick)
            island_total = island_total + inner_rate * (grad_tiles + decay_rate * master)
        average = island_total / ISLANDS
        fresh_moment = momentum_rate * moment + average
        fresh_master = master - outer_rate * (average + momentum_rate * fresh_moment)
        return fresh_master, fresh_moment

    inputs = tuple(jnp.moveaxis(array, 1, 0) for array in (gate_tiles, up_tiles, gate_where, up_where, down_where, down_global, down_moment))
    fresh_master, fresh_moment = lax.map(one_shard, inputs)
    return jnp.moveaxis(fresh_master, 0, 1), jnp.moveaxis(fresh_moment, 0, 1)
```

```python
import jax
import jax.numpy as jnp
from jax import lax
from jax.experimental import pallas as pl
from jax.experimental.pallas import tpu as pltpu
from jax.sharding import PartitionSpec as P

FF = 36864
SIDE = 128
META = 16

inner_rate = 0.5
decay_rate = 0.1
outer_rate = 0.7
momentum_rate = 0.9

f32 = jnp.float32
bf16 = jnp.bfloat16


def block(index):
    return pl.ds(pl.multiple_of(index * SIDE, SIDE), SIDE)


def local_grads(col_blocks, row_blocks, each, cells, down, tok, cot, tiles, out, gate, up, hidden_t):
    gate[...] = jnp.zeros_like(gate)
    up[...] = jnp.zeros_like(up)
    owners = tiles.shape[0]

    def project(owner, carry):
        for k in range(2 * each):
            acc = gate if k < each else up
            row = cells[owner, k]
            col = cells[owner, 2 * each + k]
            acc[col] += jnp.dot(
                tok[:, block(row)], tiles[owner, k * SIDE:(k + 1) * SIDE, :], preferred_element_type=f32
            )
        return carry

    lax.fori_loop(0, owners, project, 0)

    def activate(col, carry):
        value = gate[col]
        hidden = value / (1.0 + jnp.exp(-value)) * up[col]
        hidden_t[block(col), :] = hidden.T.astype(bf16)
        return carry

    lax.fori_loop(0, col_blocks, activate, 0)

    def reduce_tokens(group, carry):
        for k in range(8):
            j = group * 8 + k
            place = down[j]
            out[j] = jnp.dot(
                hidden_t[block(place // row_blocks), :], cot[:, block(place % row_blocks)], preferred_element_type=f32
            )
        return carry

    lax.fori_loop(0, out.shape[0] // 8, reduce_tokens, 0)


def body(tokens, cotangent, gate_tiles, up_tiles, gate_where, up_where, down_where, down_global, down_moment):
    count, width = tokens.shape
    each = gate_tiles.shape[0]
    row_blocks = width // SIDE
    col_blocks = FF // SIDE // lax.axis_size("tensor")
    fsdp = lax.axis_size("fsdp")
    kept = each * fsdp

    where = jnp.concatenate([gate_where[:, 0], up_where[:, 0]])
    cells = jnp.concatenate([where // col_blocks, where % col_blocks])
    meta = jnp.broadcast_to(cells.astype(bf16)[:, None], (META, SIDE))
    payload = jnp.concatenate([gate_tiles.reshape(each * SIDE, SIDE), up_tiles.reshape(each * SIDE, SIDE), meta])
    tiles = lax.all_gather(payload, "fsdp", axis=0)
    all_cells = tiles[:, 2 * each * SIDE:, 0].astype(jnp.int32)

    vmem = pl.BlockSpec(memory_space=pltpu.VMEM)
    smem = pl.BlockSpec(memory_space=pltpu.SMEM)
    partial = pl.pallas_call(
        lambda *refs: local_grads(col_blocks, row_blocks, each, *refs),
        out_shape=jax.ShapeDtypeStruct((kept, SIDE, SIDE), f32),
        in_specs=[smem, smem, vmem, vmem, vmem],
        out_specs=vmem,
        scratch_shapes=[
            pltpu.VMEM((col_blocks, count, SIDE), f32),
            pltpu.VMEM((col_blocks, count, SIDE), f32),
            pltpu.VMEM((col_blocks * SIDE, count), bf16),
        ],
        compiler_params=pltpu.CompilerParams(vmem_limit_bytes=48 * 2**20),
        cost_estimate=pl.CostEstimate(
            flops=2 * 3 * kept * count * SIDE * SIDE, bytes_accessed=14 * 2**20, transcendentals=col_blocks * count * SIDE
        ),
        name="local_grads",
    )(all_cells, down_where[:, 0], tokens, cotangent, tiles)

    summed = lax.psum_scatter(partial, "fsdp", scatter_dimension=0, tiled=True)
    islands = lax.axis_size("island")
    total = summed
    for bit in (1, 2):
        total = total + lax.ppermute(total, "island", [(i, i ^ bit) for i in range(islands)])
    master = down_global[:, 0]
    moment = down_moment[:, 0]
    average = inner_rate * (total / islands + decay_rate * master)
    fresh_moment = momentum_rate * moment + average
    fresh_master = master - outer_rate * (average + momentum_rate * fresh_moment)
    return (fresh_master[:, None], fresh_moment[:, None])


def solution(mesh):
    placed = (
        P(("island", "fsdp"), None),
        P(("island", "fsdp"), None),
        P("fsdp", "tensor", None, None),
        P("fsdp", "tensor", None, None),
        P("fsdp", "tensor"),
        P("fsdp", "tensor"),
        P(None, "tensor"),
        P("fsdp", "tensor", None, None),
        P("fsdp", "tensor", None, None),
    )
    return jax.shard_map(
        body,
        mesh=mesh,
        in_specs=placed,
        out_specs=(P("fsdp", "tensor", None, None), P("fsdp", "tensor", None, None)),
        check_vma=False,
    )
```

```python
import jax
import jax.numpy as jnp
from jax import lax
from jax.experimental import pallas as pl
from jax.experimental.pallas import tpu as pltpu
from jax.sharding import PartitionSpec as P

FF = 36864
SIDE = 128
META = 16
TILE_SCALE = 2.0**17
MARK = 8
TOP = 14

inner_rate = 0.5
decay_rate = 0.1
outer_rate = 0.7
momentum_rate = 0.9

f32 = jnp.float32
bf16 = jnp.bfloat16
f16 = jnp.float16


def block(index):
    return pl.ds(pl.multiple_of(index * SIDE, SIDE), SIDE)


def add_products(col_blocks, cells, tok, tiles, acc):
    owners, each = cells.shape

    def step(owner, carry):
        for k in range(each):
            cell = cells[owner, k]
            acc[cell % col_blocks] += jnp.dot(
                tok[:, block(cell // col_blocks)], tiles[owner, k * SIDE:(k + 1) * SIDE, :], preferred_element_type=f32
            )
        return carry

    lax.fori_loop(0, owners, step, 0)


def first_matrix(col_blocks, cells, tok, tiles, acc):
    acc[...] = jnp.zeros_like(acc)
    add_products(col_blocks, cells, tok, tiles, acc)


def token_sums(row_blocks, ranks, down, hidden_t, cot, out):
    halves, owners = out.shape[:2]

    def step(z, carry):
        for h in range(halves):
            place = down[z * 4 + ranks[h]]
            out[h, z] = jnp.dot(
                hidden_t[block(place // row_blocks), :], cot[:, block(place % row_blocks)], preferred_element_type=f32
            )
        return carry

    lax.fori_loop(0, owners, step, 0)


def second_matrix(col_blocks, row_blocks, cells, swapped, ranks, down, tok, tiles, first, cot, hidden_t, out, acc):
    acc[...] = jnp.zeros_like(acc)
    add_products(col_blocks, cells, tok, tiles, acc)
    first_is_gate = swapped[0] == 0

    def activate(col, carry):
        a, b = first[col], acc[col]
        gate = jnp.where(first_is_gate, a, b)
        up = jnp.where(first_is_gate, b, a)
        hidden = gate / (1.0 + jnp.exp(-gate)) * up
        hidden_t[block(col), :] = hidden.T.astype(bf16)
        return carry

    lax.fori_loop(0, col_blocks, activate, 0)
    token_sums(row_blocks, ranks, down, hidden_t, cot, out)


def call(kernel, out_shape, in_specs, scratch, flops, name):
    vmem = pl.BlockSpec(memory_space=pltpu.VMEM)
    return pl.pallas_call(
        kernel,
        out_shape=out_shape,
        in_specs=in_specs,
        out_specs=jax.tree.map(lambda _: vmem, out_shape),
        scratch_shapes=scratch,
        compiler_params=pltpu.CompilerParams(vmem_limit_bytes=20 * 2**20),
        cost_estimate=pl.CostEstimate(flops=flops, bytes_accessed=8 * 2**20, transcendentals=0),
        name=name,
    )


def narrow(values, rows):
    top = jnp.max(jnp.abs(values))
    power = jnp.clip(jnp.ceil(jnp.log2(top)), -100.0, 120.0)
    chunks = (values * jnp.exp2(TOP - power)).astype(f16).reshape(-1, rows, SIDE)
    mark = jnp.broadcast_to(power.astype(f16), (chunks.shape[0], MARK, SIDE))
    return jnp.concatenate([chunks, mark], axis=1)


def widen(chunks):
    rows = chunks.shape[1] - MARK
    power = chunks[:, rows, :1].astype(f32)
    return chunks[:, :rows].astype(f32) * jnp.exp2(power - TOP)[:, :, None]


def body(tokens, cotangent, gate_tiles, up_tiles, gate_where, up_where, down_where, down_global, down_moment):
    count, width = tokens.shape
    each = gate_tiles.shape[0]
    row_blocks = width // SIDE
    col_blocks = FF // SIDE // lax.axis_size("tensor")
    owners = lax.axis_size("fsdp")
    islands = lax.axis_size("island")
    me = lax.axis_index("island")
    core, column = me % 2, me // 2
    other_core = [(i, i ^ 1) for i in range(islands)]
    other_chip = [(i, i ^ 2) for i in range(islands)]

    is_gate = core == 0
    own = jnp.where(is_gate, gate_tiles, up_tiles).reshape(each * SIDE, SIDE)
    where = jnp.where(is_gate, gate_where, up_where)
    meta = jnp.broadcast_to(jnp.pad(where, ((0, META - each), (0, 0))).astype(f16), (META, SIDE))
    payload = jnp.concatenate([(own.astype(f32) * TILE_SCALE).astype(f16), meta])
    mine = lax.all_gather(payload, "fsdp", axis=0)
    theirs = lax.ppermute(mine, "island", other_core)

    def unpack(gathered):
        tiles = (gathered[:, :each * SIDE].astype(f32) * (1.0 / TILE_SCALE)).astype(bf16)
        return gathered[:, each * SIDE:each * SIDE + each, 0].astype(jnp.int32), tiles

    vmem = pl.BlockSpec(memory_space=pltpu.VMEM)
    smem = pl.BlockSpec(memory_space=pltpu.SMEM)
    blocks = jax.ShapeDtypeStruct((col_blocks, count, SIDE), f32)
    kept = each * owners
    down = down_where[:, 0]
    product = 2 * kept * count * SIDE * SIDE

    cells, tiles = unpack(mine)
    first = call(
        lambda *refs: first_matrix(col_blocks, *refs), blocks, [smem, vmem, vmem], [], product, "first_matrix"
    )(cells, tokens, tiles)
    cells, tiles = unpack(theirs)
    sums = jax.ShapeDtypeStruct((2, owners, SIDE, SIDE), f32)
    hidden_t, away = call(
        lambda *refs: second_matrix(col_blocks, row_blocks, *refs),
        (jax.ShapeDtypeStruct((col_blocks * SIDE, count), bf16), sums),
        [smem] * 4 + [vmem] * 4,
        [pltpu.VMEM(blocks.shape, f32)],
        product * 3 // 2,
        "second_matrix",
    )(cells, core[None], jnp.stack([column * 2 + 1 - core, (1 - column) * 2 + 1 - core]), down, tokens, tiles, first, cotangent)
    arrived = lax.ppermute(away, "island", other_core)
    stay = call(
        lambda *refs: token_sums(row_blocks, *refs), sums, [smem, smem, vmem, vmem], [], product // 2, "token_sums"
    )(jnp.stack([column * 2 + core, (1 - column) * 2 + core]), down, hidden_t, cotangent)

    chip = stay + arrived
    crossed = lax.ppermute(narrow(chip[1], owners * SIDE)[0], "island", other_chip)
    pair = chip[0] + widen(crossed[None]).reshape(owners, SIDE, SIDE)
    parts = lax.all_to_all(narrow(pair, SIDE), "fsdp", 0, 0, tiled=True)
    total = lax.all_gather(jnp.sum(widen(parts), axis=0), "island", axis=0)

    master = down_global[:, 0]
    moment = down_moment[:, 0]
    average = inner_rate * (total / islands + decay_rate * master)
    fresh_moment = momentum_rate * moment + average
    fresh_master = master - outer_rate * (average + momentum_rate * fresh_moment)
    return (fresh_master[:, None], fresh_moment[:, None])


def solution(mesh):
    placed = (
        P(("island", "fsdp"), None),
        P(("island", "fsdp"), None),
        P("fsdp", "tensor", None, None),
        P("fsdp", "tensor", None, None),
        P("fsdp", "tensor"),
        P("fsdp", "tensor"),
        P(None, "tensor"),
        P("fsdp", "tensor", None, None),
        P("fsdp", "tensor", None, None),
    )
    return jax.shard_map(
        body,
        mesh=mesh,
        in_specs=placed,
        out_specs=(P("fsdp", "tensor", None, None), P("fsdp", "tensor", None, None)),
        check_vma=False,
    )
```

```python
import functools

import jax
import jax.numpy as jnp
from jax import lax
from jax.experimental import pallas as pl
from jax.experimental.pallas import tpu as pltpu
from jax.sharding import PartitionSpec as P

FF = 36864
SIDE = 128
META = 16
TILE_SCALE = 2.0**17
MARK = 8
TOP = 14

inner_rate = 0.5
decay_rate = 0.1
outer_rate = 0.7
momentum_rate = 0.9

f32 = jnp.float32
bf16 = jnp.bfloat16
f16 = jnp.float16


def block(index):
    return pl.ds(pl.multiple_of(index * SIDE, SIDE), SIDE)


def add_products(col_blocks, cells, base, tok, sent, tiles, sems, acc):
    owners = cells.shape[0]
    each = cells.shape[1] // 2
    together = 8
    groups = owners // together

    def fetch(group):
        part = pl.ds(group * together, together)
        return pltpu.make_async_copy(sent.at[part], tiles.at[part], sems.at[group])

    for group in range(groups):
        fetch(group).start()
    acc[...] = jnp.zeros_like(acc)
    for group in range(groups):
        fetch(group).wait()
        for owner in range(group * together, (group + 1) * together):
            for k in range(each):
                cell = cells[owner, base + k]
                acc[cell % col_blocks] += jnp.dot(
                    tok[:, block(cell // col_blocks)],
                    tiles[owner, k * SIDE:(k + 1) * SIDE, :],
                    preferred_element_type=f32,
                )


def first_matrix(col_blocks, cells, base, tok, sent, acc, tiles, sems):
    add_products(col_blocks, cells, base[0], tok, sent, tiles, sems, acc)


def token_sums(row_blocks, rank, down, hidden_t, cot, out):
    for z in range(out.shape[0]):
        place = down[z * 4 + rank[0]]
        out[z] = jnp.dot(
            hidden_t[block(place // row_blocks), :], cot[:, block(place % row_blocks)], preferred_element_type=f32
        )


def second_matrix(col_blocks, row_blocks, cells, base, rank, down, sent, tok, first, cot, hidden_t, out, acc, tiles, sems):
    add_products(col_blocks, cells, base[0], tok, sent, tiles, sems, acc)
    first_is_gate = base[0] != 0
    together = 6

    def activate(group, carry):
        for near in range(together):
            col = group * together + near
            a, b = first[col], acc[col]
            gate = jnp.where(first_is_gate, a, b)
            up = jnp.where(first_is_gate, b, a)
            hidden = gate / (1.0 + jnp.exp(-gate)) * up
            hidden_t[block(col), :] = hidden.astype(bf16).T
        return carry

    lax.fori_loop(0, col_blocks // together, activate, 0)
    token_sums(row_blocks, rank, down, hidden_t, cot, out)


def call(kernel, out_shape, in_specs, scratch, flops, name):
    vmem = pl.BlockSpec(memory_space=pltpu.VMEM)
    return pl.pallas_call(
        kernel,
        out_shape=out_shape,
        in_specs=in_specs,
        out_specs=jax.tree.map(lambda _: vmem, out_shape),
        scratch_shapes=scratch,
        compiler_params=pltpu.CompilerParams(vmem_limit_bytes=18 * 2**20),
        cost_estimate=pl.CostEstimate(flops=flops, bytes_accessed=8 * 2**20, transcendentals=0),
        name=name,
    )


def narrow(values):
    top = jnp.max(jnp.abs(values))
    power = jnp.clip(jnp.ceil(jnp.log2(top)), -100.0, 120.0)
    scaled = (values * jnp.exp2(TOP - power)).astype(f16).reshape(-1, SIDE)
    return jnp.concatenate([scaled, jnp.broadcast_to(power.astype(f16), (MARK, SIDE))])


def widen(sent):
    power = sent[-1, 0].astype(f32)
    return sent[:-MARK].astype(f32) * jnp.exp2(power - TOP)


def squeeze(values):
    root = 0.5 * jnp.sqrt(jnp.abs(values))
    return jnp.where(values < 0, -root, root).astype(f16)


def stretch(sent):
    root = sent.astype(f32)
    return 4.0 * root * jnp.abs(root)


def body(tokens, cotangent, gate_tiles, up_tiles, gate_where, up_where, down_where, down_global, down_moment):
    count, width = tokens.shape
    each = gate_tiles.shape[0]
    row_blocks = width // SIDE
    col_blocks = FF // SIDE // lax.axis_size("tensor")
    owners = lax.axis_size("fsdp")
    islands = lax.axis_size("island")
    me = lax.axis_index("island")
    core, column = me % 2, me // 2
    other_core = [(i, i ^ 1) for i in range(islands)]
    other_chip = [(i, i ^ 2) for i in range(islands)]

    own = jnp.where(core == 0, gate_tiles, up_tiles).reshape(each * SIDE, SIDE)
    where = jnp.concatenate([gate_where, up_where])
    meta = jnp.broadcast_to(jnp.pad(where, ((0, META - 2 * each), (0, 0))).astype(f16), (META, SIDE))
    gathered = lax.all_gather(
        jnp.concatenate([(own.astype(f32) * TILE_SCALE).astype(f16), meta]), "fsdp", axis=0
    )
    mine = (gathered[:, :each * SIDE].astype(f32) * (1.0 / TILE_SCALE)).astype(bf16)
    theirs = lax.ppermute(mine, "island", other_core)
    cells = gathered[:, each * SIDE:each * SIDE + 2 * each, 0].astype(jnp.int32)

    vmem = pl.BlockSpec(memory_space=pltpu.VMEM)
    smem = pl.BlockSpec(memory_space=pltpu.SMEM)
    far = pl.BlockSpec(memory_space=pl.ANY)
    blocks = jax.ShapeDtypeStruct((col_blocks, count, SIDE), f32)
    sums = jax.ShapeDtypeStruct((owners, SIDE, SIDE), f32)
    kept = each * owners
    down = down_where[:, 0]
    product = 2 * kept * count * SIDE * SIDE

    def sums_of(chip, side, hidden_t):
        kernel = functools.partial(token_sums, row_blocks)
        rank = (chip * 2 + side)[None]
        return call(kernel, sums, [smem, smem, vmem, vmem], [], product // 4, "token_sums")(rank, down, hidden_t, cotangent)

    staged = pltpu.VMEM(mine.shape, bf16)
    copies = pltpu.SemaphoreType.DMA((owners // 8,))
    first = call(
        functools.partial(first_matrix, col_blocks),
        blocks,
        [smem, smem, vmem, far],
        [staged, copies],
        product,
        "first_matrix",
    )(cells, (core * each)[None], tokens, mine)
    hidden_t, away = call(
        functools.partial(second_matrix, col_blocks, row_blocks),
        (jax.ShapeDtypeStruct((col_blocks * SIDE, count), bf16), sums),
        [smem] * 4 + [far] + [vmem] * 3,
        [pltpu.VMEM(blocks.shape, f32), staged, copies],
        product * 3 // 2,
        "second_matrix",
    )(cells, ((1 - core) * each)[None], ((1 - column) * 2 + 1 - core)[None], down, theirs, tokens, first, cotangent)

    arrived = lax.ppermute(away, "island", other_core)
    leaving = sums_of(1 - column, core, hidden_t) + arrived
    crossed = lax.ppermute(narrow(leaving), "island", other_chip)
    arrived = lax.ppermute(sums_of(column, 1 - core, hidden_t), "island", other_core)
    pair = sums_of(column, core, hidden_t) + arrived + widen(crossed).reshape(sums.shape)
    parts = lax.all_to_all(squeeze(pair), "fsdp", 0, 0, tiled=True)
    total = lax.all_gather(jnp.sum(stretch(parts), axis=0), "island", axis=0)

    master = down_global[:, 0]
    moment = down_moment[:, 0]
    average = inner_rate * (total / islands + decay_rate * master)
    fresh_moment = momentum_rate * moment + average
    fresh_master = master - outer_rate * (average + momentum_rate * fresh_moment)
    return (fresh_master[:, None], fresh_moment[:, None])


def solution(mesh):
    placed = (
        P(("island", "fsdp"), None),
        P(("island", "fsdp"), None),
        P("fsdp", "tensor", None, None),
        P("fsdp", "tensor", None, None),
        P("fsdp", "tensor"),
        P("fsdp", "tensor"),
        P(None, "tensor"),
        P("fsdp", "tensor", None, None),
        P("fsdp", "tensor", None, None),
    )
    return jax.shard_map(
        body,
        mesh=mesh,
        in_specs=placed,
        out_specs=(P("fsdp", "tensor", None, None), P("fsdp", "tensor", None, None)),
        check_vma=False,
    )
```

```python
import functools

import jax
import jax.numpy as jnp
from jax import lax
from jax.experimental import pallas as pl
from jax.experimental.pallas import tpu as pltpu
from jax.sharding import PartitionSpec as P

FF = 36864
SIDE = 128
META = 16
TILE_SCALE = 2.0**17
WHOLE = 15.0

inner_rate = 0.5
decay_rate = 0.1
outer_rate = 0.7
momentum_rate = 0.9

f32 = jnp.float32
bf16 = jnp.bfloat16
f16 = jnp.float16


def block(index):
    return pl.ds(pl.multiple_of(index * SIDE, SIDE), SIDE)


def add_products(col_blocks, cells, base, tok, sent, tiles, sems, acc):
    owners = cells.shape[0]
    each = cells.shape[1] // 2
    together = 8
    groups = owners // together

    def fetch(group):
        part = pl.ds(group * together, together)
        return pltpu.make_async_copy(sent.at[part], tiles.at[part], sems.at[group])

    for group in range(groups):
        fetch(group).start()
    acc[...] = jnp.zeros_like(acc)
    for group in range(groups):
        fetch(group).wait()
        for owner in range(group * together, (group + 1) * together):
            for k in range(each):
                cell = cells[owner, base + k]
                acc[cell % col_blocks] += jnp.dot(
                    tok[:, block(cell // col_blocks)],
                    tiles[owner, k * SIDE:(k + 1) * SIDE, :],
                    preferred_element_type=f32,
                )


def first_matrix(col_blocks, cells, base, tok, sent, acc, tiles, sems):
    add_products(col_blocks, cells, base[0], tok, sent, tiles, sems, acc)


def token_sums(row_blocks, rank, down, hidden_t, cot, *refs):
    out = refs[-1]
    for z in range(out.shape[0]):
        place = down[z * 4 + rank[0]]
        out[z] = jnp.dot(
            hidden_t[block(place // row_blocks), :], cot[:, block(place % row_blocks)], preferred_element_type=f32
        )


def second_matrix(col_blocks, row_blocks, cells, base, rank, down, sent, tok, first, cot, hidden_t, out, acc, tiles, sems):
    add_products(col_blocks, cells, base[0], tok, sent, tiles, sems, acc)
    first_is_gate = base[0] != 0
    together = 6

    def activate(group, carry):
        for near in range(together):
            col = group * together + near
            a, b = first[col], acc[col]
            gate = jnp.where(first_is_gate, a, b)
            up = jnp.where(first_is_gate, b, a)
            hidden = gate / (1.0 + jnp.exp(-gate)) * up
            hidden_t[block(col), :] = hidden.astype(bf16).T
        return carry

    lax.fori_loop(0, col_blocks // together, activate, 0)
    token_sums(row_blocks, rank, down, hidden_t, cot, out)


def call(kernel, out_shape, in_specs, scratch, flops, name):
    vmem = pl.BlockSpec(memory_space=pltpu.VMEM)
    return pl.pallas_call(
        kernel,
        out_shape=out_shape,
        in_specs=in_specs,
        out_specs=jax.tree.map(lambda _: vmem, out_shape),
        scratch_shapes=scratch,
        compiler_params=pltpu.CompilerParams(vmem_limit_bytes=18 * 2**20),
        cost_estimate=pl.CostEstimate(flops=flops, bytes_accessed=8, transcendentals=0),
        name=name,
    )


def to_whole(ours, theirs, out, powers):
    owners = ours.shape[0]
    for z in range(owners):
        value = ours[z] + theirs[z]
        top = jnp.max(jnp.abs(value), axis=0, keepdims=True)
        power = jnp.floor(jnp.log2(jnp.maximum(top, 1e-30))) + 1.0
        whole = jnp.round(value * jnp.exp2(WHOLE - power))
        out[z * SIDE:(z + 1) * SIDE, :] = jnp.clip(whole, -32767.0, 32767.0).astype(jnp.int32).astype(jnp.int16)
        powers[z:z + 1, :] = power
    out[owners * SIDE:, :] = powers[...].astype(jnp.int32).astype(jnp.int16)


def from_whole(sent, owners):
    scale = jnp.exp2(sent[owners * SIDE:].astype(f32) - WHOLE)
    return sent[:owners * SIDE].reshape(owners, SIDE, SIDE).astype(f32) * scale[:, None, :]


def squeeze(values):
    root = 0.5 * jnp.sqrt(jnp.abs(values))
    return jnp.where(values < 0, -root, root).astype(f16)


def stretch(sent):
    root = sent.astype(f32)
    return 4.0 * root * jnp.abs(root)


def body(tokens, cotangent, gate_tiles, up_tiles, gate_where, up_where, down_where, down_global, down_moment):
    count, width = tokens.shape
    each = gate_tiles.shape[0]
    row_blocks = width // SIDE
    col_blocks = FF // SIDE // lax.axis_size("tensor")
    owners = lax.axis_size("fsdp")
    islands = lax.axis_size("island")
    me = lax.axis_index("island")
    core, column = me % 2, me // 2
    other_core = [(i, i ^ 1) for i in range(islands)]
    other_chip = [(i, i ^ 2) for i in range(islands)]

    own = jnp.where(core == 0, gate_tiles, up_tiles).reshape(each * SIDE, SIDE)
    where = jnp.concatenate([gate_where, up_where])
    meta = jnp.broadcast_to(jnp.pad(where, ((0, META - 2 * each), (0, 0))).astype(f32), (META, SIDE))
    payload = jnp.concatenate([own.astype(f32) * TILE_SCALE, meta]).astype(f16)
    gathered = lax.all_gather(payload, "fsdp", axis=0)
    mine = (gathered[:, :each * SIDE].astype(f32) * (1.0 / TILE_SCALE)).astype(bf16)
    theirs = lax.ppermute(mine, "island", other_core)
    cells = gathered[:, each * SIDE:each * SIDE + 2 * each, 0].astype(jnp.int32)

    vmem = pl.BlockSpec(memory_space=pltpu.VMEM)
    smem = pl.BlockSpec(memory_space=pltpu.SMEM)
    far = pl.BlockSpec(memory_space=pl.ANY)
    blocks = jax.ShapeDtypeStruct((col_blocks, count, SIDE), f32)
    sums = jax.ShapeDtypeStruct((owners, SIDE, SIDE), f32)
    kept = each * owners
    down = down_where[:, 0]
    product = 2 * kept * count * SIDE * SIDE

    def sums_of(chip, side, *after):
        kernel = functools.partial(token_sums, row_blocks)
        rank = (chip * 2 + side)[None]
        return call(kernel, sums, [smem, smem, vmem, vmem] + [far] * len(after), [], 10**11, "token_sums")(
            rank, down, hidden_t, cotangent, *after
        )

    staged = pltpu.VMEM(mine.shape, bf16)
    copies = pltpu.SemaphoreType.DMA((owners // 8,))
    first = call(
        functools.partial(first_matrix, col_blocks),
        blocks,
        [smem, smem, vmem, far],
        [staged, copies],
        product,
        "first_matrix",
    )(cells, (core * each)[None], tokens, mine)
    hidden_t, away = call(
        functools.partial(second_matrix, col_blocks, row_blocks),
        (jax.ShapeDtypeStruct((col_blocks * SIDE, count), bf16), sums),
        [smem] * 4 + [far] + [vmem] * 3,
        [pltpu.VMEM(blocks.shape, f32), staged, copies],
        product * 3 // 2,
        "second_matrix",
    )(cells, ((1 - core) * each)[None], ((1 - column) * 2 + 1 - core)[None], down, theirs, tokens, first, cotangent)

    arrived = lax.ppermute(away, "island", other_core)
    leaving = call(
        to_whole,
        jax.ShapeDtypeStruct(((SIDE + 1) * owners, SIDE), jnp.int16),
        [vmem, vmem],
        [pltpu.VMEM((owners, SIDE), f32)],
        product // 4,
        "to_whole",
    )(sums_of(1 - column, core), arrived)
    crossed = lax.ppermute(leaving, "island", other_chip)
    arrived = lax.ppermute(sums_of(column, 1 - core, leaving), "island", other_core)
    pair = sums_of(column, core, leaving) + arrived + from_whole(crossed, owners)
    parts = lax.all_to_all(squeeze(pair), "fsdp", 0, 0, tiled=True)
    total = lax.all_gather(jnp.sum(stretch(parts), axis=0), "island", axis=0)

    master = down_global[:, 0]
    moment = down_moment[:, 0]
    average = inner_rate * (total / islands + decay_rate * master)
    fresh_moment = momentum_rate * moment + average
    fresh_master = master - outer_rate * (average + momentum_rate * fresh_moment)
    return (fresh_master[:, None], fresh_moment[:, None])


def solution(mesh):
    placed = (
        P(("island", "fsdp"), None),
        P(("island", "fsdp"), None),
        P("fsdp", "tensor", None, None),
        P("fsdp", "tensor", None, None),
        P("fsdp", "tensor"),
        P("fsdp", "tensor"),
        P(None, "tensor"),
        P("fsdp", "tensor", None, None),
        P("fsdp", "tensor", None, None),
    )
    return jax.shard_map(
        body,
        mesh=mesh,
        in_specs=placed,
        out_specs=(P("fsdp", "tensor", None, None), P("fsdp", "tensor", None, None)),
        check_vma=False,
    )
```

```python
import functools

import jax
import jax.numpy as jnp
from jax import lax
from jax.experimental import pallas as pl
from jax.experimental.pallas import tpu as pltpu
from jax.sharding import PartitionSpec as P

FF = 36864
SIDE = 128
TILE_SCALE = 2.0**17
WHOLE = 15.0

inner_rate = 0.5
decay_rate = 0.1
outer_rate = 0.7
momentum_rate = 0.9

f32 = jnp.float32
bf16 = jnp.bfloat16
f16 = jnp.float16


def block(index):
    return pl.ds(pl.multiple_of(index * SIDE, SIDE), SIDE)


def add_products(cells, base, tok, sent, tiles, sems, acc):
    owners = cells.shape[0]
    each = cells.shape[1] // 4
    together = 4
    groups = owners // together

    def fetch(group):
        part = pl.ds(group * together, together)
        return pltpu.make_async_copy(sent.at[part, pl.ds(0, each * SIDE)], tiles.at[part], sems.at[group])

    for group in range(groups):
        fetch(group).start()
    acc[...] = jnp.zeros_like(acc)
    for group in range(groups):
        fetch(group).wait()
        for owner in range(group * together, (group + 1) * together):
            for k in range(each):
                acc[cells[owner, 2 * each + base + k]] += jnp.dot(
                    tok[:, block(cells[owner, base + k])],
                    tiles[owner, k * SIDE:(k + 1) * SIDE, :],
                    preferred_element_type=f32,
                )


def first_matrix(cells, base, tok, sent, acc, tiles, sems):
    add_products(cells, base[0], tok, sent, tiles, sems, acc)


def token_sums(row_blocks, rank, down, hidden_t, cot, *refs):
    out = refs[-1]
    for z in range(out.shape[0]):
        place = down[z * 4 + rank[0]]
        out[z] = jnp.dot(
            hidden_t[block(place // row_blocks), :], cot[:, block(place % row_blocks)], preferred_element_type=f32
        )


def second_matrix(col_blocks, row_blocks, cells, base, rank, down, sent, tok, first, cot, hidden_t, out, acc, tiles, sems):
    add_products(cells, base[0], tok, sent, tiles, sems, acc)
    first_is_gate = base[0] != 0
    together = 6

    def activate(group, carry):
        for near in range(together):
            col = group * together + near
            a, b = first[col], acc[col]
            gate = jnp.where(first_is_gate, a, b)
            up = jnp.where(first_is_gate, b, a)
            hidden = gate / (1.0 + jnp.exp(-gate)) * up
            hidden_t[block(col), :] = hidden.astype(bf16).T
        return carry

    lax.fori_loop(0, col_blocks // together, activate, 0)
    token_sums(row_blocks, rank, down, hidden_t, cot, out)


def call(kernel, out_shape, in_specs, scratch, flops, name):
    vmem = pl.BlockSpec(memory_space=pltpu.VMEM)
    return pl.pallas_call(
        kernel,
        out_shape=out_shape,
        in_specs=in_specs,
        out_specs=jax.tree.map(lambda _: vmem, out_shape),
        scratch_shapes=scratch,
        compiler_params=pltpu.CompilerParams(vmem_limit_bytes=18 * 2**20),
        cost_estimate=pl.CostEstimate(flops=flops, bytes_accessed=8, transcendentals=0),
        name=name,
    )


def to_whole(ours, theirs, out, powers):
    owners = ours.shape[0]
    for z in range(owners):
        value = ours[z] + theirs[z]
        top = jnp.max(jnp.abs(value), axis=0, keepdims=True)
        power = jnp.floor(jnp.log2(jnp.maximum(top, 1e-30))) + 1.0
        whole = jnp.round(value * jnp.exp2(WHOLE - power))
        out[z * SIDE:(z + 1) * SIDE, :] = jnp.clip(whole, -32767.0, 32767.0).astype(jnp.int32).astype(jnp.int16)
        powers[z:z + 1, :] = power
    out[owners * SIDE:, :] = powers[...].astype(jnp.int32).astype(jnp.int16)


def from_whole(ours, theirs, sent, out, scales):
    owners = ours.shape[0]
    scales[...] = jnp.exp2(sent[owners * SIDE:, :].astype(jnp.int32).astype(f32) - WHOLE)
    for z in range(owners):
        whole = sent[z * SIDE:(z + 1) * SIDE, :].astype(jnp.int32).astype(f32)
        value = ours[z] + theirs[z] + whole * scales[z:z + 1, :]
        root = 0.5 * jnp.sqrt(jnp.abs(value))
        out[z] = jnp.where(value < 0, -root, root)


def stretch(sent):
    root = sent.astype(f32)
    return 4.0 * root * jnp.abs(root)


def body(tokens, cotangent, gate_tiles, up_tiles, gate_where, up_where, down_where, down_global, down_moment):
    count, width = tokens.shape
    each = gate_tiles.shape[0]
    row_blocks = width // SIDE
    col_blocks = FF // SIDE // lax.axis_size("tensor")
    owners = lax.axis_size("fsdp")
    islands = lax.axis_size("island")
    me = lax.axis_index("island")
    core, column = me % 2, me // 2
    other_core = [(i, i ^ 1) for i in range(islands)]
    other_chip = [(i, i ^ 2) for i in range(islands)]

    own = jnp.where(core == 0, gate_tiles, up_tiles).reshape(each * SIDE, SIDE)
    where = jnp.concatenate([gate_where, up_where])
    where = jnp.concatenate([where // col_blocks, where % col_blocks])
    meta = jnp.broadcast_to(where.astype(f32), (4 * each, SIDE))
    payload = jnp.concatenate([own.astype(f32) * TILE_SCALE, meta]).astype(f16)
    gathered = lax.all_gather(payload, "fsdp", axis=0)
    mine = (gathered.astype(f32) * (1.0 / TILE_SCALE)).astype(bf16)
    cells = (mine[:, each * SIDE:, 0].astype(f32) * TILE_SCALE).astype(jnp.int32)
    theirs = lax.ppermute(mine, "island", other_core)

    vmem = pl.BlockSpec(memory_space=pltpu.VMEM)
    smem = pl.BlockSpec(memory_space=pltpu.SMEM)
    far = pl.BlockSpec(memory_space=pl.ANY)
    blocks = jax.ShapeDtypeStruct((col_blocks, count, SIDE), f32)
    sums = jax.ShapeDtypeStruct((owners, SIDE, SIDE), f32)
    kept = each * owners
    down = down_where[:, 0]
    product = 2 * kept * count * SIDE * SIDE

    def sums_of(chip, side, *after):
        kernel = functools.partial(token_sums, row_blocks)
        rank = (chip * 2 + side)[None]
        return call(kernel, sums, [smem, smem, vmem, vmem] + [far] * len(after), [], 10**11, "token_sums")(
            rank, down, hidden_t, cotangent, *after
        )

    staged = pltpu.VMEM((owners, each * SIDE, SIDE), bf16)
    copies = pltpu.SemaphoreType.DMA((owners // 4,))
    first = call(
        first_matrix,
        blocks,
        [smem, smem, vmem, far],
        [staged, copies],
        product,
        "first_matrix",
    )(cells, (core * each)[None], tokens, mine)
    hidden_t, away = call(
        functools.partial(second_matrix, col_blocks, row_blocks),
        (jax.ShapeDtypeStruct((col_blocks * SIDE, count), bf16), sums),
        [smem] * 4 + [far] + [vmem] * 3,
        [pltpu.VMEM(blocks.shape, f32), staged, copies],
        product * 3 // 2,
        "second_matrix",
    )(cells, ((1 - core) * each)[None], ((1 - column) * 2 + 1 - core)[None], down, theirs, tokens, first, cotangent)

    arrived = lax.ppermute(away, "island", other_core)
    leaving = call(
        to_whole,
        jax.ShapeDtypeStruct(((SIDE + 1) * owners, SIDE), jnp.int16),
        [vmem, vmem],
        [pltpu.VMEM((owners, SIDE), f32)],
        product // 4,
        "to_whole",
    )(sums_of(1 - column, core), arrived)
    crossed = lax.ppermute(leaving, "island", other_chip)
    arrived = lax.ppermute(sums_of(column, 1 - core, leaving), "island", other_core)
    roots = call(
        from_whole, sums, [vmem] * 3, [pltpu.VMEM((owners, SIDE), f32)], product // 4, "from_whole"
    )(sums_of(column, core, leaving), arrived, crossed)
    parts = lax.all_to_all(roots.astype(f16), "fsdp", 0, 0, tiled=True)
    total = lax.all_gather(jnp.sum(stretch(parts), axis=0), "island", axis=0)

    master = down_global[:, 0]
    moment = down_moment[:, 0]
    average = inner_rate * (total / islands + decay_rate * master)
    fresh_moment = momentum_rate * moment + average
    fresh_master = master - outer_rate * (average + momentum_rate * fresh_moment)
    return (fresh_master[:, None], fresh_moment[:, None])


def solution(mesh):
    placed = (
        P(("island", "fsdp"), None),
        P(("island", "fsdp"), None),
        P("fsdp", "tensor", None, None),
        P("fsdp", "tensor", None, None),
        P("fsdp", "tensor"),
        P("fsdp", "tensor"),
        P(None, "tensor"),
        P("fsdp", "tensor", None, None),
        P("fsdp", "tensor", None, None),
    )
    return jax.shard_map(
        body,
        mesh=mesh,
        in_specs=placed,
        out_specs=(P("fsdp", "tensor", None, None), P("fsdp", "tensor", None, None)),
        check_vma=False,
    )
```

```python
import functools

import jax
import jax.numpy as jnp
from jax import lax
from jax.experimental import pallas as pl
from jax.experimental.pallas import tpu as pltpu
from jax.sharding import PartitionSpec as P

FF = 36864
SIDE = 128
TILE_SCALE = 2.0**17
WHOLE = 15.0

inner_rate = 0.5
decay_rate = 0.1
outer_rate = 0.7
momentum_rate = 0.9

f32 = jnp.float32
bf16 = jnp.bfloat16
f16 = jnp.float16


def block(index):
    return pl.ds(pl.multiple_of(index * SIDE, SIDE), SIDE)


def add_products(cells, base, tok, sent, tiles, sems, acc):
    owners = cells.shape[0]
    each = cells.shape[1] // 4
    together = 4
    groups = owners // together

    def fetch(group):
        part = pl.ds(group * together, together)
        return pltpu.make_async_copy(sent.at[part, pl.ds(0, each * SIDE)], tiles.at[part], sems.at[group])

    for group in range(groups):
        fetch(group).start()
    acc[...] = jnp.zeros_like(acc)
    for group in range(groups):
        fetch(group).wait()
        for owner in range(group * together, (group + 1) * together):
            for k in range(each):
                acc[cells[owner, 2 * each + base + k]] += jnp.dot(
                    tok[:, block(cells[owner, base + k])],
                    tiles[owner, k * SIDE:(k + 1) * SIDE, :],
                    preferred_element_type=f32,
                )


def first_matrix(cells, base, tok, sent, acc, tiles, sems):
    add_products(cells, base[0], tok, sent, tiles, sems, acc)


def token_sums(row_blocks, side, down, hidden_t, cot, out):
    columns, owners = out.shape[:2]
    for h in range(columns):
        for z in range(owners):
            place = down[z * 4 + h * 2 + side[0]]
            out[h, z] = jnp.dot(
                hidden_t[block(place // row_blocks), :], cot[:, block(place % row_blocks)], preferred_element_type=f32
            )


def second_matrix(col_blocks, row_blocks, cells, base, side, down, sent, tok, first, cot, hidden_t, out, acc, tiles, sems):
    add_products(cells, base[0], tok, sent, tiles, sems, acc)
    first_is_gate = base[0] != 0
    together = 6

    def activate(group, carry):
        for near in range(together):
            col = group * together + near
            a, b = first[col], acc[col]
            gate = jnp.where(first_is_gate, a, b)
            up = jnp.where(first_is_gate, b, a)
            hidden = gate / (1.0 + jnp.exp(-gate)) * up
            hidden_t[block(col), :] = hidden.astype(bf16).T
        return carry

    lax.fori_loop(0, col_blocks // together, activate, 0)
    token_sums(row_blocks, side, down, hidden_t, cot, out)


def call(kernel, out_shape, in_specs, scratch, flops, name):
    vmem = pl.BlockSpec(memory_space=pltpu.VMEM)
    return pl.pallas_call(
        kernel,
        out_shape=out_shape,
        in_specs=in_specs,
        out_specs=jax.tree.map(lambda _: vmem, out_shape),
        scratch_shapes=scratch,
        compiler_params=pltpu.CompilerParams(vmem_limit_bytes=18 * 2**20),
        cost_estimate=pl.CostEstimate(flops=flops, bytes_accessed=8, transcendentals=0),
        name=name,
    )


def to_whole(ours, theirs, out, powers):
    columns, owners = ours.shape[:2]
    half = SIDE // 2
    for h in range(columns):
        for b in range(2):
            chunk = 2 * h + b
            for z in range(owners):
                rows = slice(b * half, (b + 1) * half)
                value = ours[h, z, rows, :] + theirs[h, z, rows, :]
                top = jnp.max(jnp.abs(value), axis=0, keepdims=True)
                power = jnp.floor(jnp.log2(jnp.maximum(top, 1e-30))) + 1.0
                whole = jnp.clip(jnp.round(value * jnp.exp2(WHOLE - power)), -32767.0, 32767.0)
                out[chunk, z * half:(z + 1) * half, :] = whole.astype(jnp.int32).astype(jnp.int16)
                powers[z:z + 1, :] = power
            out[chunk, owners * half:, :] = powers[...].astype(jnp.int32).astype(jnp.int16)


def from_whole(sent, out, scales):
    chunks = sent.shape[0]
    owners, half = out.shape[:2]
    for k in range(chunks):
        scales[k] = jnp.exp2(sent[k, owners * half:, :].astype(jnp.int32).astype(f32) - WHOLE)
    for z in range(owners):
        value = jnp.zeros((half, SIDE), f32)
        for k in range(chunks):
            value += sent[k, z * half:(z + 1) * half, :].astype(jnp.int32).astype(f32) * scales[k, z:z + 1, :]
        root = 0.25 * jnp.sqrt(jnp.abs(value))
        out[z] = jnp.where(value < 0, -root, root)


def stretch(sent):
    root = sent.astype(f32)
    return 16.0 * root * jnp.abs(root)


def body(tokens, cotangent, gate_tiles, up_tiles, gate_where, up_where, down_where, down_global, down_moment):
    count, width = tokens.shape
    each = gate_tiles.shape[0]
    row_blocks = width // SIDE
    col_blocks = FF // SIDE // lax.axis_size("tensor")
    owners = lax.axis_size("fsdp")
    islands = lax.axis_size("island")
    me = lax.axis_index("island")
    core = me % 2
    other_core = [(i, i ^ 1) for i in range(islands)]
    fours = [
        [(2 * h + c) * owners + 2 * q + b for h in range(2) for b in range(2)] for c in range(2) for q in range(owners // 2)
    ]

    own = jnp.where(core == 0, gate_tiles, up_tiles).reshape(each * SIDE, SIDE)
    where = jnp.concatenate([gate_where, up_where])
    where = jnp.concatenate([where // col_blocks, where % col_blocks])
    meta = jnp.broadcast_to(where.astype(f32), (4 * each, SIDE))
    payload = jnp.concatenate([own.astype(f32) * TILE_SCALE, meta]).astype(f16)
    gathered = lax.all_gather(payload, "fsdp", axis=0)
    mine = (gathered.astype(f32) * (1.0 / TILE_SCALE)).astype(bf16)
    cells = (mine[:, each * SIDE:, 0].astype(f32) * TILE_SCALE).astype(jnp.int32)
    theirs = lax.ppermute(mine, "island", other_core)

    vmem = pl.BlockSpec(memory_space=pltpu.VMEM)
    smem = pl.BlockSpec(memory_space=pltpu.SMEM)
    far = pl.BlockSpec(memory_space=pl.ANY)
    blocks = jax.ShapeDtypeStruct((col_blocks, count, SIDE), f32)
    sums = jax.ShapeDtypeStruct((2, owners, SIDE, SIDE), f32)
    kept = each * owners
    down = down_where[:, 0]
    product = 2 * kept * count * SIDE * SIDE

    staged = pltpu.VMEM((owners, each * SIDE, SIDE), bf16)
    copies = pltpu.SemaphoreType.DMA((owners // 4,))
    first = call(
        first_matrix,
        blocks,
        [smem, smem, vmem, far],
        [staged, copies],
        product,
        "first_matrix",
    )(cells, (core * each)[None], tokens, mine)
    hidden_t, away = call(
        functools.partial(second_matrix, col_blocks, row_blocks),
        (jax.ShapeDtypeStruct((col_blocks * SIDE, count), bf16), sums),
        [smem] * 4 + [far] + [vmem] * 3,
        [pltpu.VMEM(blocks.shape, f32), staged, copies],
        product * 3 // 2,
        "second_matrix",
    )(cells, ((1 - core) * each)[None], (1 - core)[None], down, theirs, tokens, first, cotangent)

    arrived = lax.ppermute(away, "island", other_core)
    stay = call(
        functools.partial(token_sums, row_blocks), sums, [smem, smem, vmem, vmem], [], 10**11, "token_sums"
    )(core[None], down, hidden_t, cotangent)
    half = SIDE // 2
    leaving = call(
        to_whole,
        jax.ShapeDtypeStruct((4, (half + 1) * owners, SIDE), jnp.int16),
        [vmem, vmem],
        [pltpu.VMEM((owners, SIDE), f32)],
        product // 4,
        "to_whole",
    )(stay, arrived)
    crossed = lax.all_to_all(leaving, ("island", "fsdp"), 0, 0, tiled=True, axis_index_groups=fours)
    roots = call(
        from_whole,
        jax.ShapeDtypeStruct((owners, half, SIDE), f32),
        [vmem],
        [pltpu.VMEM((4, owners, SIDE), f32)],
        product // 4,
        "from_whole",
    )(crossed)
    parts = lax.all_to_all(roots.astype(f16), "fsdp", 0, 0, tiled=True)
    tile = jnp.sum(stretch(parts).reshape(owners // 2, 2, half, SIDE), axis=0).reshape(SIDE, SIDE)
    total = lax.all_gather(tile, "island", axis=0)

    master = down_global[:, 0]
    moment = down_moment[:, 0]
    average = inner_rate * (total / islands + decay_rate * master)
    fresh_moment = momentum_rate * moment + average
    fresh_master = master - outer_rate * (average + momentum_rate * fresh_moment)
    return (fresh_master[:, None], fresh_moment[:, None])


def solution(mesh):
    placed = (
        P(("island", "fsdp"), None),
        P(("island", "fsdp"), None),
        P("fsdp", "tensor", None, None),
        P("fsdp", "tensor", None, None),
        P("fsdp", "tensor"),
        P("fsdp", "tensor"),
        P(None, "tensor"),
        P("fsdp", "tensor", None, None),
        P("fsdp", "tensor", None, None),
    )
    return jax.shard_map(
        body,
        mesh=mesh,
        in_specs=placed,
        out_specs=(P("fsdp", "tensor", None, None), P("fsdp", "tensor", None, None)),
        check_vma=False,
    )
```

```python
import functools

import jax
import jax.numpy as jnp
from jax import lax
from jax.experimental import pallas as pl
from jax.experimental.pallas import tpu as pltpu
from jax.sharding import PartitionSpec as P

FF = 36864
SIDE = 128
TILE_SCALE = 2.0**17
WHOLE = 15.0
MARK = 16

inner_rate = 0.5
decay_rate = 0.1
outer_rate = 0.7
momentum_rate = 0.9

f32 = jnp.float32
bf16 = jnp.bfloat16
f16 = jnp.float16
s16 = jnp.int16


def block(index):
    return pl.ds(pl.multiple_of(index * SIDE, SIDE), SIDE)


def add_products(cells, base, tok, sent, tiles, sems, acc):
    owners = cells.shape[0]
    each = cells.shape[1] // 4
    together = 4
    groups = owners // together

    def fetch(group):
        part = pl.ds(group * together, together)
        return pltpu.make_async_copy(sent.at[part, pl.ds(0, each * SIDE)], tiles.at[part], sems.at[group])

    for group in range(groups):
        fetch(group).start()
    acc[...] = jnp.zeros_like(acc)
    for group in range(groups):
        fetch(group).wait()
        for owner in range(group * together, (group + 1) * together):
            for k in range(each):
                acc[cells[owner, 2 * each + base + k]] += jnp.dot(
                    tok[:, block(cells[owner, base + k])],
                    tiles[owner, k * SIDE:(k + 1) * SIDE, :],
                    preferred_element_type=f32,
                )


def first_matrix(cells, base, tok, sent, acc, tiles, sems):
    add_products(cells, base[0], tok, sent, tiles, sems, acc)


def to_whole(value):
    top = jnp.max(jnp.abs(value), axis=0, keepdims=True)
    power = jnp.floor(jnp.log2(jnp.maximum(top, 1e-30))) + 1.0
    whole = jnp.clip(jnp.round(value * jnp.exp2(WHOLE - power)), -32767.0, 32767.0)
    return whole.astype(jnp.int32).astype(s16), power


def wide(whole):
    return whole.astype(jnp.int32).astype(f32)


def scale_of(powers):
    return jnp.exp2(wide(powers) - WHOLE)


def token_sum(row_blocks, place, hidden_t, cot):
    return jnp.dot(
        hidden_t[block(place // row_blocks), :], cot[:, block(place % row_blocks)], preferred_element_type=f32
    )


def keep_sums(row_blocks, side, down, hidden_t, cot, out):
    columns, owners = out.shape[:2]
    for h in range(columns):
        for z in range(owners):
            out[h, z] = token_sum(row_blocks, down[z * 4 + h * 2 + side[0]], hidden_t, cot)


def second_matrix(
    col_blocks, row_blocks, cells, base, side, down, sent, tok, first, cot, hidden_t, out, acc, tiles, sems, powers
):
    add_products(cells, base[0], tok, sent, tiles, sems, acc)
    first_is_gate = base[0] != 0
    together = 6

    def activate(group, carry):
        for near in range(together):
            col = group * together + near
            a, b = first[col], acc[col]
            gate = jnp.where(first_is_gate, a, b)
            up = jnp.where(first_is_gate, b, a)
            hidden = gate / (1.0 + jnp.exp(-gate)) * up
            hidden_t[block(col), :] = hidden.astype(bf16).T
        return carry

    lax.fori_loop(0, col_blocks // together, activate, 0)
    count = powers.shape[0]
    owners = count // 2
    for t in range(count):
        place = down[t % owners * 4 + t // owners * 2 + side[0]]
        whole, power = to_whole(token_sum(row_blocks, place, hidden_t, cot))
        out[t * SIDE:(t + 1) * SIDE, :] = whole
        powers[t:t + 1, :] = power
    out[count * SIDE:, :] = powers[...].astype(jnp.int32).astype(s16)


def call(kernel, out_shape, in_specs, scratch, flops, name):
    vmem = pl.BlockSpec(memory_space=pltpu.VMEM)
    return pl.pallas_call(
        kernel,
        out_shape=out_shape,
        in_specs=in_specs,
        out_specs=jax.tree.map(lambda _: vmem, out_shape),
        scratch_shapes=scratch,
        compiler_params=pltpu.CompilerParams(vmem_limit_bytes=18 * 2**20),
        cost_estimate=pl.CostEstimate(flops=flops, bytes_accessed=8, transcendentals=0),
        name=name,
    )


def add_cores(ours, theirs, out, scales, powers):
    columns, owners = ours.shape[:2]
    half = SIDE // 2
    scales[...] = scale_of(theirs[columns * owners * SIDE:, :])
    for h in range(columns):
        for b in range(2):
            chunk = 2 * h + b
            for z in range(owners):
                t = h * owners + z
                start = t * SIDE + b * half
                value = ours[h, z, b * half:(b + 1) * half, :] + wide(theirs[start:start + half, :]) * scales[t:t + 1, :]
                whole, power = to_whole(value)
                out[chunk, z * half:(z + 1) * half, :] = whole
                powers[z:z + 1, :] = power
            out[chunk, owners * half:, :] = powers[...].astype(jnp.int32).astype(s16)


def add_fours(sent, out, scales):
    chunks = sent.shape[0]
    owners = out.shape[0]
    half = SIDE // 2
    for k in range(chunks):
        scales[k] = scale_of(sent[k, owners * half:, :])
    for z in range(owners):
        value = jnp.zeros((half, SIDE), f32)
        for k in range(chunks):
            value += wide(sent[k, z * half:(z + 1) * half, :]) * scales[k, z:z + 1, :]
        whole, power = to_whole(value)
        out[z, :half, :] = whole
        out[z, half:, :] = jnp.broadcast_to(power, (MARK, SIDE)).astype(jnp.int32).astype(s16)


def add_ring(sent, out):
    owners = sent.shape[0]
    half = SIDE // 2
    for b in range(2):
        value = jnp.zeros((half, SIDE), f32)
        for z in range(b, owners, 2):
            value += wide(sent[z, :half, :]) * scale_of(sent[z, half:, :])[:1, :]
        out[b * half:(b + 1) * half, :] = value


def body(tokens, cotangent, gate_tiles, up_tiles, gate_where, up_where, down_where, down_global, down_moment):
    count, width = tokens.shape
    each = gate_tiles.shape[0]
    row_blocks = width // SIDE
    col_blocks = FF // SIDE // lax.axis_size("tensor")
    owners = lax.axis_size("fsdp")
    islands = lax.axis_size("island")
    me = lax.axis_index("island")
    core = me % 2
    other_core = [(i, i ^ 1) for i in range(islands)]
    fours = [
        [(2 * h + c) * owners + 2 * q + b for h in range(2) for b in range(2)] for c in range(2) for q in range(owners // 2)
    ]

    own = jnp.where(core == 0, gate_tiles, up_tiles).reshape(each * SIDE, SIDE)
    where = jnp.concatenate([gate_where, up_where])
    where = jnp.concatenate([where // col_blocks, where % col_blocks])
    meta = jnp.broadcast_to(where.astype(f32), (4 * each, SIDE))
    payload = jnp.concatenate([own.astype(f32) * TILE_SCALE, meta]).astype(f16)
    gathered = lax.all_gather(payload, "fsdp", axis=0)
    mine = (gathered.astype(f32) * (1.0 / TILE_SCALE)).astype(bf16)
    cells = (mine[:, each * SIDE:, 0].astype(f32) * TILE_SCALE).astype(jnp.int32)
    theirs = lax.ppermute(mine, "island", other_core)

    vmem = pl.BlockSpec(memory_space=pltpu.VMEM)
    smem = pl.BlockSpec(memory_space=pltpu.SMEM)
    far = pl.BlockSpec(memory_space=pl.ANY)
    blocks = jax.ShapeDtypeStruct((col_blocks, count, SIDE), f32)
    sums = jax.ShapeDtypeStruct((2, owners, SIDE, SIDE), f32)
    kept = each * owners
    down = down_where[:, 0]
    product = 2 * kept * count * SIDE * SIDE

    staged = pltpu.VMEM((owners, each * SIDE, SIDE), bf16)
    copies = pltpu.SemaphoreType.DMA((owners // 4,))
    first = call(
        first_matrix,
        blocks,
        [smem, smem, vmem, far],
        [staged, copies],
        product,
        "first_matrix",
    )(cells, (core * each)[None], tokens, mine)
    hidden_t, away = call(
        functools.partial(second_matrix, col_blocks, row_blocks),
        (jax.ShapeDtypeStruct((col_blocks * SIDE, count), bf16), jax.ShapeDtypeStruct(((SIDE + 1) * 2 * owners, SIDE), s16)),
        [smem] * 4 + [far] + [vmem] * 3,
        [pltpu.VMEM(blocks.shape, f32), staged, copies, pltpu.VMEM((2 * owners, SIDE), f32)],
        product * 3 // 2,
        "second_matrix",
    )(cells, ((1 - core) * each)[None], (1 - core)[None], down, theirs, tokens, first, cotangent)

    arrived = lax.ppermute(away, "island", other_core)
    stay = call(
        functools.partial(keep_sums, row_blocks), sums, [smem, smem, vmem, vmem], [], 10**11, "keep_sums"
    )(core[None], down, hidden_t, cotangent)
    half = SIDE // 2
    leaving = call(
        add_cores,
        jax.ShapeDtypeStruct((4, (half + 1) * owners, SIDE), s16),
        [vmem, vmem],
        [pltpu.VMEM((2 * owners, SIDE), f32), pltpu.VMEM((owners, SIDE), f32)],
        product // 4,
        "add_cores",
    )(stay, arrived)
    crossed = lax.all_to_all(leaving, ("island", "fsdp"), 0, 0, tiled=True, axis_index_groups=fours)
    halves = call(
        add_fours,
        jax.ShapeDtypeStruct((owners, half + MARK, SIDE), s16),
        [vmem],
        [pltpu.VMEM((4, owners, SIDE), f32)],
        product // 4,
        "add_fours",
    )(crossed)
    parts = lax.all_to_all(halves, "fsdp", 0, 0, tiled=True)
    tile = call(add_ring, jax.ShapeDtypeStruct((SIDE, SIDE), f32), [vmem], [], product // 4, "add_ring")(parts)
    total = lax.all_gather(tile, "island", axis=0)

    master = down_global[:, 0]
    moment = down_moment[:, 0]
    average = inner_rate * (total / islands + decay_rate * master)
    fresh_moment = momentum_rate * moment + average
    fresh_master = master - outer_rate * (average + momentum_rate * fresh_moment)
    return (fresh_master[:, None], fresh_moment[:, None])


def solution(mesh):
    placed = (
        P(("island", "fsdp"), None),
        P(("island", "fsdp"), None),
        P("fsdp", "tensor", None, None),
        P("fsdp", "tensor", None, None),
        P("fsdp", "tensor"),
        P("fsdp", "tensor"),
        P(None, "tensor"),
        P("fsdp", "tensor", None, None),
        P("fsdp", "tensor", None, None),
    )
    return jax.shard_map(
        body,
        mesh=mesh,
        in_specs=placed,
        out_specs=(P("fsdp", "tensor", None, None), P("fsdp", "tensor", None, None)),
        check_vma=False,
    )
```

```python
import functools

import jax
import jax.numpy as jnp
from jax import lax
from jax.experimental import pallas as pl
from jax.experimental.pallas import tpu as pltpu
from jax.sharding import PartitionSpec as P

FF = 36864
SIDE = 128
TILE_SCALE = 2.0**17
WHOLE = 15.0

inner_rate = 0.5
decay_rate = 0.1
outer_rate = 0.7
momentum_rate = 0.9

f32 = jnp.float32
bf16 = jnp.bfloat16
f16 = jnp.float16
s16 = jnp.int16


def block(index):
    return pl.ds(pl.multiple_of(index * SIDE, SIDE), SIDE)


def add_products(cells, base, tok, sent, tiles, sems, acc):
    owners = cells.shape[0]
    each = cells.shape[1] // 4
    together = 4
    groups = owners // together

    def fetch(group):
        part = pl.ds(group * together, together)
        return pltpu.make_async_copy(sent.at[part, pl.ds(0, each * SIDE)], tiles.at[part], sems.at[group])

    for group in range(groups):
        fetch(group).start()
    acc[...] = jnp.zeros_like(acc)
    for group in range(groups):
        fetch(group).wait()
        for owner in range(group * together, (group + 1) * together):
            for k in range(each):
                acc[cells[owner, 2 * each + base + k]] += jnp.dot(
                    tok[:, block(cells[owner, base + k])],
                    tiles[owner, k * SIDE:(k + 1) * SIDE, :],
                    preferred_element_type=f32,
                )


def first_matrix(cells, base, tok, sent, acc, tiles, sems):
    add_products(cells, base[0], tok, sent, tiles, sems, acc)


def to_whole(value):
    top = jnp.max(jnp.abs(value), axis=0, keepdims=True)
    power = jnp.floor(jnp.log2(jnp.maximum(top, 1e-30))) + 1.0
    whole = jnp.clip(jnp.round(value * jnp.exp2(WHOLE - power)), -32767.0, 32767.0)
    return whole.astype(jnp.int32).astype(s16), power


def wide(whole):
    return whole.astype(jnp.int32).astype(f32)


def scale_of(powers):
    return jnp.exp2(wide(powers) - WHOLE)


def token_sum(row_blocks, place, hidden_t, cot):
    return jnp.dot(
        hidden_t[block(place // row_blocks), :], cot[:, block(place % row_blocks)], preferred_element_type=f32
    )


def keep_sums(row_blocks, side, down, hidden_t, cot, out):
    columns, owners = out.shape[:2]
    for h in range(columns):
        for z in range(owners):
            out[h, z] = token_sum(row_blocks, down[z * 4 + h * 2 + side[0]], hidden_t, cot)


def second_matrix(
    col_blocks, row_blocks, cells, base, side, down, sent, tok, first, cot, hidden_t, out, acc, tiles, sems, powers
):
    add_products(cells, base[0], tok, sent, tiles, sems, acc)
    first_is_gate = base[0] != 0
    together = 6

    def activate(group, carry):
        for near in range(together):
            col = group * together + near
            a, b = first[col], acc[col]
            gate = jnp.where(first_is_gate, a, b)
            up = jnp.where(first_is_gate, b, a)
            hidden = gate / (1.0 + jnp.exp(-gate)) * up
            hidden_t[block(col), :] = hidden.astype(bf16).T
        return carry

    lax.fori_loop(0, col_blocks // together, activate, 0)
    count = powers.shape[0]
    owners = count // 2
    for t in range(count):
        place = down[t % owners * 4 + t // owners * 2 + side[0]]
        whole, power = to_whole(token_sum(row_blocks, place, hidden_t, cot))
        out[t * SIDE:(t + 1) * SIDE, :] = whole
        powers[t:t + 1, :] = power
    out[count * SIDE:, :] = powers[...].astype(jnp.int32).astype(s16)


def call(kernel, out_shape, in_specs, scratch, flops, name):
    vmem = pl.BlockSpec(memory_space=pltpu.VMEM)
    return pl.pallas_call(
        kernel,
        out_shape=out_shape,
        in_specs=in_specs,
        out_specs=jax.tree.map(lambda _: vmem, out_shape),
        scratch_shapes=scratch,
        compiler_params=pltpu.CompilerParams(vmem_limit_bytes=18 * 2**20),
        cost_estimate=pl.CostEstimate(flops=flops, bytes_accessed=8, transcendentals=0),
        name=name,
    )


def add_cores(ours, theirs, out, scales, powers):
    columns, owners = ours.shape[:2]
    half = SIDE // 2
    scales[...] = scale_of(theirs[columns * owners * SIDE:, :])
    for h in range(columns):
        for b in range(2):
            chunk = 2 * h + b
            for z in range(owners):
                t = h * owners + z
                start = t * SIDE + b * half
                value = ours[h, z, b * half:(b + 1) * half, :] + wide(theirs[start:start + half, :]) * scales[t:t + 1, :]
                whole, power = to_whole(value)
                out[chunk, z * half:(z + 1) * half, :] = whole
                powers[z:z + 1, :] = power
            out[chunk, owners * half:, :] = powers[...].astype(jnp.int32).astype(s16)


def add_fours(sent, out, scales):
    chunks = sent.shape[0]
    owners, half = out.shape[:2]
    for k in range(chunks):
        scales[k] = scale_of(sent[k, owners * half:, :])
    for z in range(owners):
        value = jnp.zeros((half, SIDE), f32)
        for k in range(chunks):
            value += wide(sent[k, z * half:(z + 1) * half, :]) * scales[k, z:z + 1, :]
        root = 0.25 * jnp.sqrt(jnp.abs(value))
        out[z] = jnp.where(value < 0, -root, root)


def stretch(sent):
    root = sent.astype(f32)
    return 16.0 * root * jnp.abs(root)


def body(tokens, cotangent, gate_tiles, up_tiles, gate_where, up_where, down_where, down_global, down_moment):
    count, width = tokens.shape
    each = gate_tiles.shape[0]
    row_blocks = width // SIDE
    col_blocks = FF // SIDE // lax.axis_size("tensor")
    owners = lax.axis_size("fsdp")
    islands = lax.axis_size("island")
    me = lax.axis_index("island")
    core = me % 2
    other_core = [(i, i ^ 1) for i in range(islands)]
    fours = [
        [(2 * h + c) * owners + 2 * q + b for h in range(2) for b in range(2)] for c in range(2) for q in range(owners // 2)
    ]

    own = jnp.where(core == 0, gate_tiles, up_tiles).reshape(each * SIDE, SIDE)
    where = jnp.concatenate([gate_where, up_where])
    where = jnp.concatenate([where // col_blocks, where % col_blocks])
    meta = jnp.broadcast_to(where.astype(f32), (4 * each, SIDE))
    payload = jnp.concatenate([own.astype(f32) * TILE_SCALE, meta]).astype(f16)
    gathered = lax.all_gather(payload, "fsdp", axis=0)
    mine = (gathered.astype(f32) * (1.0 / TILE_SCALE)).astype(bf16)
    cells = (mine[:, each * SIDE:, 0].astype(f32) * TILE_SCALE).astype(jnp.int32)
    theirs = lax.ppermute(mine, "island", other_core)

    vmem = pl.BlockSpec(memory_space=pltpu.VMEM)
    smem = pl.BlockSpec(memory_space=pltpu.SMEM)
    far = pl.BlockSpec(memory_space=pl.ANY)
    blocks = jax.ShapeDtypeStruct((col_blocks, count, SIDE), f32)
    sums = jax.ShapeDtypeStruct((2, owners, SIDE, SIDE), f32)
    kept = each * owners
    down = down_where[:, 0]
    product = 2 * kept * count * SIDE * SIDE

    staged = pltpu.VMEM((owners, each * SIDE, SIDE), bf16)
    copies = pltpu.SemaphoreType.DMA((owners // 4,))
    first = call(
        first_matrix,
        blocks,
        [smem, smem, vmem, far],
        [staged, copies],
        product,
        "first_matrix",
    )(cells, (core * each)[None], tokens, mine)
    hidden_t, away = call(
        functools.partial(second_matrix, col_blocks, row_blocks),
        (jax.ShapeDtypeStruct((col_blocks * SIDE, count), bf16), jax.ShapeDtypeStruct(((SIDE + 1) * 2 * owners, SIDE), s16)),
        [smem] * 4 + [far] + [vmem] * 3,
        [pltpu.VMEM(blocks.shape, f32), staged, copies, pltpu.VMEM((2 * owners, SIDE), f32)],
        product * 3 // 2,
        "second_matrix",
    )(cells, ((1 - core) * each)[None], (1 - core)[None], down, theirs, tokens, first, cotangent)

    arrived = lax.ppermute(away, "island", other_core)
    stay = call(
        functools.partial(keep_sums, row_blocks), sums, [smem, smem, vmem, vmem], [], 10**11, "keep_sums"
    )(core[None], down, hidden_t, cotangent)
    half = SIDE // 2
    leaving = call(
        add_cores,
        jax.ShapeDtypeStruct((4, (half + 1) * owners, SIDE), s16),
        [vmem, vmem],
        [pltpu.VMEM((2 * owners, SIDE), f32), pltpu.VMEM((owners, SIDE), f32)],
        product // 4,
        "add_cores",
    )(stay, arrived)
    crossed = lax.all_to_all(leaving, ("island", "fsdp"), 0, 0, tiled=True, axis_index_groups=fours)
    roots = call(
        add_fours,
        jax.ShapeDtypeStruct((owners, half, SIDE), f32),
        [vmem],
        [pltpu.VMEM((4, owners, SIDE), f32)],
        product // 4,
        "add_fours",
    )(crossed)
    parts = lax.all_to_all(roots.astype(f16), "fsdp", 0, 0, tiled=True)
    tile = jnp.sum(stretch(parts).reshape(owners // 2, 2, half, SIDE), axis=0).reshape(SIDE, SIDE)
    total = lax.all_gather(tile, "island", axis=0)

    master = down_global[:, 0]
    moment = down_moment[:, 0]
    average = inner_rate * (total / islands + decay_rate * master)
    fresh_moment = momentum_rate * moment + average
    fresh_master = master - outer_rate * (average + momentum_rate * fresh_moment)
    return (fresh_master[:, None], fresh_moment[:, None])


def solution(mesh):
    placed = (
        P(("island", "fsdp"), None),
        P(("island", "fsdp"), None),
        P("fsdp", "tensor", None, None),
        P("fsdp", "tensor", None, None),
        P("fsdp", "tensor"),
        P("fsdp", "tensor"),
        P(None, "tensor"),
        P("fsdp", "tensor", None, None),
        P("fsdp", "tensor", None, None),
    )
    return jax.shard_map(
        body,
        mesh=mesh,
        in_specs=placed,
        out_specs=(P("fsdp", "tensor", None, None), P("fsdp", "tensor", None, None)),
        check_vma=False,
    )
```

```python
import functools

import jax
import jax.numpy as jnp
from jax import lax
from jax.experimental import pallas as pl
from jax.experimental.pallas import tpu as pltpu
from jax.sharding import PartitionSpec as P

FF = 36864
SIDE = 128
TILE_SCALE = 2.0**17
WHOLE = 15.0

inner_rate = 0.5
decay_rate = 0.1
outer_rate = 0.7
momentum_rate = 0.9

f32 = jnp.float32
bf16 = jnp.bfloat16
f16 = jnp.float16
s16 = jnp.int16


def block(index):
    return pl.ds(pl.multiple_of(index * SIDE, SIDE), SIDE)


def add_products(cells, base, tok, sent, tiles, sems, acc):
    owners = cells.shape[0]
    each = cells.shape[1] // 4
    together = 2
    groups = owners // together

    def fetch(group):
        part = pl.ds(group * together, together)
        return pltpu.make_async_copy(sent.at[part, pl.ds(0, each * SIDE)], tiles.at[part], sems.at[group])

    for group in range(groups):
        fetch(group).start()
    acc[...] = jnp.zeros_like(acc)
    for group in range(groups):
        fetch(group).wait()
        for owner in range(group * together, (group + 1) * together):
            for k in range(each):
                acc[cells[owner, 2 * each + base + k]] += jnp.dot(
                    tok[:, block(cells[owner, base + k])],
                    tiles[owner, k * SIDE:(k + 1) * SIDE, :],
                    preferred_element_type=f32,
                )


def first_matrix(cells, base, tok, sent, acc, tiles, sems):
    add_products(cells, base[0], tok, sent, tiles, sems, acc)


def to_whole(value):
    top = jnp.max(jnp.abs(value), axis=0, keepdims=True)
    power = jnp.floor(jnp.log2(jnp.maximum(top, 1e-30))) + 1.0
    whole = jnp.clip(jnp.round(value * jnp.exp2(WHOLE - power)), -32767.0, 32767.0)
    return whole.astype(jnp.int32).astype(s16), power


def wide(whole):
    return whole.astype(jnp.int32).astype(f32)


def scale_of(powers):
    return jnp.exp2(wide(powers) - WHOLE)


def token_sum(row_blocks, place, hidden_t, cot):
    return jnp.dot(
        hidden_t[block(place // row_blocks), :], cot[:, block(place % row_blocks)], preferred_element_type=f32
    )


def keep_sums(row_blocks, side, down, hidden_t, cot, out):
    columns, owners = out.shape[:2]
    for h in range(columns):
        for z in range(owners):
            out[h, z] = token_sum(row_blocks, down[z * 4 + h * 2 + side[0]], hidden_t, cot)


def second_matrix(
    col_blocks, row_blocks, cells, base, side, down, sent, tok, first, cot, hidden_t, out, acc, tiles, sems, powers
):
    add_products(cells, base[0], tok, sent, tiles, sems, acc)
    first_is_gate = base[0] != 0
    together = 9

    def activate(group, carry):
        for near in range(together):
            col = group * together + near
            a, b = first[col], acc[col]
            gate = jnp.where(first_is_gate, a, b)
            up = jnp.where(first_is_gate, b, a)
            hidden = gate / (1.0 + jnp.exp(-gate)) * up
            hidden_t[block(col), :] = hidden.astype(bf16).T
        return carry

    lax.fori_loop(0, col_blocks // together, activate, 0)
    count = powers.shape[0]
    owners = count // 2
    for t in range(count):
        place = down[t % owners * 4 + t // owners * 2 + side[0]]
        whole, power = to_whole(token_sum(row_blocks, place, hidden_t, cot))
        out[t * SIDE:(t + 1) * SIDE, :] = whole
        powers[t:t + 1, :] = power
    out[count * SIDE:, :] = powers[...].astype(jnp.int32).astype(s16)


def call(kernel, out_shape, in_specs, scratch, flops, name):
    vmem = pl.BlockSpec(memory_space=pltpu.VMEM)
    return pl.pallas_call(
        kernel,
        out_shape=out_shape,
        in_specs=in_specs,
        out_specs=jax.tree.map(lambda _: vmem, out_shape),
        scratch_shapes=scratch,
        compiler_params=pltpu.CompilerParams(vmem_limit_bytes=18 * 2**20),
        cost_estimate=pl.CostEstimate(flops=flops, bytes_accessed=8, transcendentals=0),
        name=name,
    )


def add_cores(ours, theirs, out, scales, powers):
    columns, owners = ours.shape[:2]
    half = SIDE // 2
    scales[...] = scale_of(theirs[columns * owners * SIDE:, :])
    for h in range(columns):
        for b in range(2):
            chunk = 2 * h + b
            for z in range(owners):
                t = h * owners + z
                start = t * SIDE + b * half
                value = ours[h, z, b * half:(b + 1) * half, :] + wide(theirs[start:start + half, :]) * scales[t:t + 1, :]
                whole, power = to_whole(value)
                out[chunk, z * half:(z + 1) * half, :] = whole
                powers[z:z + 1, :] = power
            out[chunk, owners * half:, :] = powers[...].astype(jnp.int32).astype(s16)


def add_fours(sent, out, scales):
    chunks = sent.shape[0]
    owners, half = out.shape[:2]
    for k in range(chunks):
        scales[k] = scale_of(sent[k, owners * half:, :])
    for z in range(owners):
        value = jnp.zeros((half, SIDE), f32)
        for k in range(chunks):
            value += wide(sent[k, z * half:(z + 1) * half, :]) * scales[k, z:z + 1, :]
        root = 0.25 * jnp.sqrt(jnp.abs(value))
        out[z] = jnp.where(value < 0, -root, root)


def stretch(sent):
    root = sent.astype(f32)
    return 16.0 * root * jnp.abs(root)


def body(tokens, cotangent, gate_tiles, up_tiles, gate_where, up_where, down_where, down_global, down_moment):
    count, width = tokens.shape
    each = gate_tiles.shape[0]
    row_blocks = width // SIDE
    col_blocks = FF // SIDE // lax.axis_size("tensor")
    owners = lax.axis_size("fsdp")
    islands = lax.axis_size("island")
    me = lax.axis_index("island")
    core = me % 2
    other_core = [(i, i ^ 1) for i in range(islands)]
    fours = [
        [(2 * h + c) * owners + 2 * q + b for h in range(2) for b in range(2)] for c in range(2) for q in range(owners // 2)
    ]

    own = jnp.where(core == 0, gate_tiles, up_tiles).reshape(each * SIDE, SIDE)
    where = jnp.concatenate([gate_where, up_where])
    where = jnp.concatenate([where // col_blocks, where % col_blocks])
    meta = jnp.broadcast_to(where.astype(f32), (4 * each, SIDE))
    payload = jnp.concatenate([own.astype(f32) * TILE_SCALE, meta]).astype(f16)
    gathered = lax.all_gather(payload, "fsdp", axis=0)
    mine = (gathered.astype(f32) * (1.0 / TILE_SCALE)).astype(bf16)
    cells = (mine[:, each * SIDE:, 0].astype(f32) * TILE_SCALE).astype(jnp.int32)
    theirs = lax.ppermute(mine, "island", other_core)

    vmem = pl.BlockSpec(memory_space=pltpu.VMEM)
    smem = pl.BlockSpec(memory_space=pltpu.SMEM)
    far = pl.BlockSpec(memory_space=pl.ANY)
    blocks = jax.ShapeDtypeStruct((col_blocks, count, SIDE), f32)
    sums = jax.ShapeDtypeStruct((2, owners, SIDE, SIDE), f32)
    kept = each * owners
    down = down_where[:, 0]
    product = 2 * kept * count * SIDE * SIDE

    staged = pltpu.VMEM((owners, each * SIDE, SIDE), bf16)
    copies = pltpu.SemaphoreType.DMA((owners // 2,))
    first = call(
        first_matrix,
        blocks,
        [smem, smem, vmem, far],
        [staged, copies],
        product,
        "first_matrix",
    )(cells, (core * each)[None], tokens, mine)
    hidden_t, away = call(
        functools.partial(second_matrix, col_blocks, row_blocks),
        (jax.ShapeDtypeStruct((col_blocks * SIDE, count), bf16), jax.ShapeDtypeStruct(((SIDE + 1) * 2 * owners, SIDE), s16)),
        [smem] * 4 + [far] + [vmem] * 3,
        [pltpu.VMEM(blocks.shape, f32), staged, copies, pltpu.VMEM((2 * owners, SIDE), f32)],
        product * 3 // 2,
        "second_matrix",
    )(cells, ((1 - core) * each)[None], (1 - core)[None], down, theirs, tokens, first, cotangent)

    arrived = lax.ppermute(away, "island", other_core)
    stay = call(
        functools.partial(keep_sums, row_blocks), sums, [smem, smem, vmem, vmem], [], 10**11, "keep_sums"
    )(core[None], down, hidden_t, cotangent)
    half = SIDE // 2
    leaving = call(
        add_cores,
        jax.ShapeDtypeStruct((4, (half + 1) * owners, SIDE), s16),
        [vmem, vmem],
        [pltpu.VMEM((2 * owners, SIDE), f32), pltpu.VMEM((owners, SIDE), f32)],
        product // 4,
        "add_cores",
    )(stay, arrived)
    crossed = lax.all_to_all(leaving, ("island", "fsdp"), 0, 0, tiled=True, axis_index_groups=fours)
    roots = call(
        add_fours,
        jax.ShapeDtypeStruct((owners, half, SIDE), f32),
        [vmem],
        [pltpu.VMEM((4, owners, SIDE), f32)],
        product // 4,
        "add_fours",
    )(crossed)
    parts = lax.all_to_all(roots.astype(f16), "fsdp", 0, 0, tiled=True)
    tile = jnp.sum(stretch(parts).reshape(owners // 2, 2, half, SIDE), axis=0).reshape(SIDE, SIDE)
    total = lax.all_gather(tile, "island", axis=0)

    master = down_global[:, 0]
    moment = down_moment[:, 0]
    average = inner_rate * (total / islands + decay_rate * master)
    fresh_moment = momentum_rate * moment + average
    fresh_master = master - outer_rate * (average + momentum_rate * fresh_moment)
    return (fresh_master[:, None], fresh_moment[:, None])


def solution(mesh):
    placed = (
        P(("island", "fsdp"), None),
        P(("island", "fsdp"), None),
        P("fsdp", "tensor", None, None),
        P("fsdp", "tensor", None, None),
        P("fsdp", "tensor"),
        P("fsdp", "tensor"),
        P(None, "tensor"),
        P("fsdp", "tensor", None, None),
        P("fsdp", "tensor", None, None),
    )
    return jax.shard_map(
        body,
        mesh=mesh,
        in_specs=placed,
        out_specs=(P("fsdp", "tensor", None, None), P("fsdp", "tensor", None, None)),
        check_vma=False,
    )
```

```python
import functools

import jax
import jax.numpy as jnp
from jax import lax
from jax.experimental import pallas as pl
from jax.experimental.pallas import tpu as pltpu
from jax.sharding import PartitionSpec as P

FF = 36864
SIDE = 128
TILE_SCALE = 2.0**17
WHOLE = 15.0

inner_rate = 0.5
decay_rate = 0.1
outer_rate = 0.7
momentum_rate = 0.9

f32 = jnp.float32
bf16 = jnp.bfloat16
f16 = jnp.float16
s16 = jnp.int16


def block(index):
    return pl.ds(pl.multiple_of(index * SIDE, SIDE), SIDE)


def add_products(cells, base, tok, sent, tiles, sems, acc):
    owners = cells.shape[0]
    each = cells.shape[1] // 4
    together = 8
    groups = owners // together

    def fetch(group):
        part = pl.ds(group * together, together)
        return pltpu.make_async_copy(sent.at[part, pl.ds(0, each * SIDE)], tiles.at[part], sems.at[group])

    for group in range(groups):
        fetch(group).start()
    acc[...] = jnp.zeros_like(acc)
    for group in range(groups):
        fetch(group).wait()
        for owner in range(group * together, (group + 1) * together):
            for k in range(each):
                acc[cells[owner, 2 * each + base + k]] += jnp.dot(
                    tok[:, block(cells[owner, base + k])],
                    tiles[owner, k * SIDE:(k + 1) * SIDE, :],
                    preferred_element_type=f32,
                )


def first_matrix(cells, base, tok, sent, acc, tiles, sems):
    add_products(cells, base[0], tok, sent, tiles, sems, acc)


def to_whole(value):
    top = jnp.max(jnp.abs(value), axis=0, keepdims=True)
    power = jnp.floor(jnp.log2(jnp.maximum(top, 1e-30))) + 1.0
    whole = jnp.clip(jnp.round(value * jnp.exp2(WHOLE - power)), -32767.0, 32767.0)
    return whole.astype(jnp.int32).astype(s16), power


def wide(whole):
    return whole.astype(jnp.int32).astype(f32)


def scale_of(powers):
    return jnp.exp2(wide(powers) - WHOLE)


def token_sum(row_blocks, place, hidden_t, cot):
    return jnp.dot(
        hidden_t[block(place // row_blocks), :], cot[:, block(place % row_blocks)], preferred_element_type=f32
    )


def keep_sums(row_blocks, side, down, hidden_t, cot, out):
    columns, owners = out.shape[:2]
    for h in range(columns):
        for z in range(owners):
            out[h, z] = token_sum(row_blocks, down[z * 4 + h * 2 + side[0]], hidden_t, cot)


def second_matrix(
    col_blocks, row_blocks, cells, base, side, down, sent, tok, first, cot, hidden_t, out, acc, tiles, sems, powers
):
    add_products(cells, base[0], tok, sent, tiles, sems, acc)
    first_is_gate = base[0] != 0
    together = 9

    def activate(group, carry):
        for near in range(together):
            col = group * together + near
            a, b = first[col], acc[col]
            gate = jnp.where(first_is_gate, a, b)
            up = jnp.where(first_is_gate, b, a)
            hidden = gate / (1.0 + jnp.exp(-gate)) * up
            hidden_t[block(col), :] = hidden.astype(bf16).T
        return carry

    lax.fori_loop(0, col_blocks // together, activate, 0)
    count = powers.shape[0]
    owners = count // 2
    for t in range(count):
        place = down[t % owners * 4 + t // owners * 2 + side[0]]
        whole, power = to_whole(token_sum(row_blocks, place, hidden_t, cot))
        out[t * SIDE:(t + 1) * SIDE, :] = whole
        powers[t:t + 1, :] = power
    out[count * SIDE:, :] = powers[...].astype(jnp.int32).astype(s16)


def call(kernel, out_shape, in_specs, scratch, flops, name):
    vmem = pl.BlockSpec(memory_space=pltpu.VMEM)
    return pl.pallas_call(
        kernel,
        out_shape=out_shape,
        in_specs=in_specs,
        out_specs=jax.tree.map(lambda _: vmem, out_shape),
        scratch_shapes=scratch,
        compiler_params=pltpu.CompilerParams(vmem_limit_bytes=18 * 2**20),
        cost_estimate=pl.CostEstimate(flops=flops, bytes_accessed=8, transcendentals=0),
        name=name,
    )


def add_cores(ours, theirs, out, scales, powers):
    columns, owners = ours.shape[:2]
    half = SIDE // 2
    scales[...] = scale_of(theirs[columns * owners * SIDE:, :])
    for h in range(columns):
        for b in range(2):
            chunk = 2 * h + b
            for z in range(owners):
                t = h * owners + z
                start = t * SIDE + b * half
                value = ours[h, z, b * half:(b + 1) * half, :] + wide(theirs[start:start + half, :]) * scales[t:t + 1, :]
                whole, power = to_whole(value)
                out[chunk, z * half:(z + 1) * half, :] = whole
                powers[z:z + 1, :] = power
            out[chunk, owners * half:, :] = powers[...].astype(jnp.int32).astype(s16)


def add_fours(sent, out, scales):
    chunks = sent.shape[0]
    owners, half = out.shape[:2]
    for k in range(chunks):
        scales[k] = scale_of(sent[k, owners * half:, :])
    for z in range(owners):
        value = jnp.zeros((half, SIDE), f32)
        for k in range(chunks):
            value += wide(sent[k, z * half:(z + 1) * half, :]) * scales[k, z:z + 1, :]
        root = 0.25 * jnp.sqrt(jnp.abs(value))
        out[z] = jnp.where(value < 0, -root, root)


def stretch(sent):
    root = sent.astype(f32)
    return 16.0 * root * jnp.abs(root)


def body(tokens, cotangent, gate_tiles, up_tiles, gate_where, up_where, down_where, down_global, down_moment):
    count, width = tokens.shape
    each = gate_tiles.shape[0]
    row_blocks = width // SIDE
    col_blocks = FF // SIDE // lax.axis_size("tensor")
    owners = lax.axis_size("fsdp")
    islands = lax.axis_size("island")
    me = lax.axis_index("island")
    core = me % 2
    other_core = [(i, i ^ 1) for i in range(islands)]
    fours = [
        [(2 * h + c) * owners + 2 * q + b for h in range(2) for b in range(2)] for c in range(2) for q in range(owners // 2)
    ]

    own = jnp.where(core == 0, gate_tiles, up_tiles).reshape(each * SIDE, SIDE)
    where = jnp.concatenate([gate_where, up_where])
    where = jnp.concatenate([where // col_blocks, where % col_blocks])
    meta = jnp.broadcast_to(where.astype(f32), (4 * each, SIDE))
    payload = jnp.concatenate([own.astype(f32) * TILE_SCALE, meta]).astype(f16)
    gathered = lax.all_gather(payload, "fsdp", axis=0)
    mine = (gathered.astype(f32) * (1.0 / TILE_SCALE)).astype(bf16)
    cells = (mine[:, each * SIDE:, 0].astype(f32) * TILE_SCALE).astype(jnp.int32)
    theirs = lax.ppermute(mine, "island", other_core)

    vmem = pl.BlockSpec(memory_space=pltpu.VMEM)
    smem = pl.BlockSpec(memory_space=pltpu.SMEM)
    far = pl.BlockSpec(memory_space=pl.ANY)
    blocks = jax.ShapeDtypeStruct((col_blocks, count, SIDE), f32)
    sums = jax.ShapeDtypeStruct((2, owners, SIDE, SIDE), f32)
    kept = each * owners
    down = down_where[:, 0]
    product = 2 * kept * count * SIDE * SIDE

    staged = pltpu.VMEM((owners, each * SIDE, SIDE), bf16)
    copies = pltpu.SemaphoreType.DMA((owners // 8,))
    first = call(
        first_matrix,
        blocks,
        [smem, smem, vmem, far],
        [staged, copies],
        product,
        "first_matrix",
    )(cells, (core * each)[None], tokens, mine)
    hidden_t, away = call(
        functools.partial(second_matrix, col_blocks, row_blocks),
        (jax.ShapeDtypeStruct((col_blocks * SIDE, count), bf16), jax.ShapeDtypeStruct(((SIDE + 1) * 2 * owners, SIDE), s16)),
        [smem] * 4 + [far] + [vmem] * 3,
        [pltpu.VMEM(blocks.shape, f32), staged, copies, pltpu.VMEM((2 * owners, SIDE), f32)],
        product * 3 // 2,
        "second_matrix",
    )(cells, ((1 - core) * each)[None], (1 - core)[None], down, theirs, tokens, first, cotangent)

    arrived = lax.ppermute(away, "island", other_core)
    stay = call(
        functools.partial(keep_sums, row_blocks), sums, [smem, smem, vmem, vmem], [], 10**11, "keep_sums"
    )(core[None], down, hidden_t, cotangent)
    half = SIDE // 2
    leaving = call(
        add_cores,
        jax.ShapeDtypeStruct((4, (half + 1) * owners, SIDE), s16),
        [vmem, vmem],
        [pltpu.VMEM((2 * owners, SIDE), f32), pltpu.VMEM((owners, SIDE), f32)],
        product // 4,
        "add_cores",
    )(stay, arrived)
    crossed = lax.all_to_all(leaving, ("island", "fsdp"), 0, 0, tiled=True, axis_index_groups=fours)
    roots = call(
        add_fours,
        jax.ShapeDtypeStruct((owners, half, SIDE), f32),
        [vmem],
        [pltpu.VMEM((4, owners, SIDE), f32)],
        product // 4,
        "add_fours",
    )(crossed)
    parts = lax.all_to_all(roots.astype(f16), "fsdp", 0, 0, tiled=True)
    tile = jnp.sum(stretch(parts).reshape(owners // 2, 2, half, SIDE), axis=0).reshape(SIDE, SIDE)
    total = lax.all_gather(tile, "island", axis=0)

    master = down_global[:, 0]
    moment = down_moment[:, 0]
    average = inner_rate * (total / islands + decay_rate * master)
    fresh_moment = momentum_rate * moment + average
    fresh_master = master - outer_rate * (average + momentum_rate * fresh_moment)
    return (fresh_master[:, None], fresh_moment[:, None])


def solution(mesh):
    placed = (
        P(("island", "fsdp"), None),
        P(("island", "fsdp"), None),
        P("fsdp", "tensor", None, None),
        P("fsdp", "tensor", None, None),
        P("fsdp", "tensor"),
        P("fsdp", "tensor"),
        P(None, "tensor"),
        P("fsdp", "tensor", None, None),
        P("fsdp", "tensor", None, None),
    )
    return jax.shard_map(
        body,
        mesh=mesh,
        in_specs=placed,
        out_specs=(P("fsdp", "tensor", None, None), P("fsdp", "tensor", None, None)),
        check_vma=False,
    )
```
